256 devices in a mesh: dp: 8 (over z_lo, y), expert: 32 (over z_hi, x, core).
Axes of the slice: x: 4, y: 4, z: 8 (z_hi: 4, z_lo: 2; z = z_hi * 2 + z_lo), core: 2. Of those that a mesh axis runs over, the one named last changes fastest.
Arguments:
- tokens: bfloat16 [32768, 2048], P(('dp', 'expert')), may hold values from -6 to 6
- grad_out: bfloat16 [32768, 2048], P(('dp', 'expert')), may hold values from -1.5 to 1.5
- routes: int32 [32768, 2], P(('dp', 'expert')), may hold values from 0 to 31, all different within a row; in each aligned block of 128 rows (0 to 127, 128 to 255, ...) at most 16 rows name the same one
- gate_fixed: int32 [32768, 2], P(('dp', 'expert')), may hold values from 26 to 256
- live_count: int32 [256], P(('dp', 'expert')), may hold values from 1 to 128, 28672 in all
- w_gate: bfloat16 [32, 2048, 768], P('expert', 'dp'), may hold values from -0.125 to 0.125
- w_up: bfloat16 [32, 2048, 768], P('expert', 'dp'), may hold values from -0.125 to 0.125
- w_down: bfloat16 [32, 768, 2048], P('expert', None, 'dp'), may hold values from -0.21875 to 0.21875
Outputs:
- d_tokens: bfloat16 [32768, 2048], P(('dp', 'expert'))
- d_gates: bfloat16 [32768, 2], P(('dp', 'expert'))
- grad_gate: bfloat16 [32, 2048, 768], P('expert', 'dp')
- grad_up: bfloat16 [32, 2048, 768], P('expert', 'dp')
- grad_down: bfloat16 [32, 768, 2048], P('expert', None, 'dp')
The draws below stay inside these ranges and needn't reach their ends.
Inputs may be any that keep to these rules, and one draw needn't show every extreme that they name: `routes`: each row names 2 different experts; among the rows of one device no expert is named more than 16 times. `live_count`: a device's live tokens are its first rows; the largest count equals 128.
All inputs are finite; a program needn't handle non-finite values.
Results may differ from the reference program's by a relative error of at most 0.017.
Values may be sent and summed in bfloat16 or wider, within the bound.
No kernel may reach another device: no remote copies, remote signals or barrier semaphores. Data moves between devices by JAX's collectives and lax.ppermute only.
A program may use at most 128 MiB of HBM per device.

```python
import math
import jax
import jax.numpy as jnp
import numpy as np
from jax import lax

D = 2048
FF = 768
TOP = 2
TOK_DEV = 128
EXPERTS = 32
TOKENS = 32768
CAP = 16
LIVE = 28672
N_DP = 8
N_EXPERT = 32
DEVICES = 256


def plant(drawn, own_key, smallest, high):
    place = [jax.random.randint(jax.random.fold_in(own_key, axis), (), 0, length) for axis, length in enumerate(drawn.shape)]
    main_axis = drawn.shape.index(max(drawn.shape))
    beside = place[:main_axis] + [(place[main_axis] + 1) % drawn.shape[main_axis]] + place[main_axis + 1:]
    return drawn.at[tuple(place)].set(smallest).at[tuple(beside)].set(high)


def block_scale(stream_key, dims, split, smallest, largest):
    factor_of = 1.0
    for axis_at, shards_of in split:
        steps = jax.random.uniform(jax.random.fold_in(jax.random.fold_in(stream_key, 6), axis_at), (shards_of,), jnp.float32, smallest / len(split), largest / len(split))
        factor_of = factor_of * jnp.repeat(jnp.exp(steps), dims[axis_at] // shards_of).reshape((-1,) + (1,) * (len(dims) - 1 - axis_at))
    return factor_of


def split_up(number_of, total, bound, slope):
    weights = [(1 << 20) // math.isqrt(rank ** slope) + 1 for rank in range(2, number_of + 1)]
    spare, holding = total - bound - (number_of - 1), [1] * (number_of - 1)
    while spare > 0:
        free = [i for i in range(number_of - 1) if holding[i] < bound]
        pool, remaining = sum([weights[i] for i in free]), spare
        for i in free:
            more = min(bound - holding[i], max(1, remaining * weights[i] // pool), spare)
            holding[i] = holding[i] + more
            spare = spare - more
    return np.array([bound] + holding)


def uneven_parts(rng, count, total, bound, slope):
    if count == 2:
        one = jax.random.randint(rng, (), max(1, total - bound), min(bound, total - 1) + 1)
        return jnp.stack([one, total - one])
    lengths = jnp.asarray(split_up(count, total, bound, slope), jnp.int32)
    twos = (count - 1) // 2
    donor, sink = lengths[1:1 + 2 * twos:2], lengths[2:2 + 2 * twos:2]
    slack = jnp.minimum(donor - 1, bound - sink)
    shifted = jax.random.randint(jax.random.fold_in(rng, 1), (twos,), 0, 1 << 20) % (slack + 1)
    lengths = lengths.at[1:1 + 2 * twos:2].set(donor - shifted).at[2:2 + 2 * twos:2].set(sink + shifted)
    return lengths[jax.random.permutation(jax.random.fold_in(rng, 2), count)]


def shared_out(stream_key, own, number, rows, number_of, top, limit, skew):
    sequence = jax.random.permutation(stream_key, number_of)
    heavy_load, ordinary = shares(number_of, rows * top, limit, skew, True), shares(number_of, rows * top, limit, skew, False)
    places = jnp.arange(number_of)

    def named(lengths, offset_by):
        used = int((lengths > 0).sum())
        fixed = max(1, used // 4)
        shifted = fixed + (places - fixed + offset_by * (used - fixed)) % max(1, number_of - fixed)
        return jnp.zeros((number_of,), jnp.int32).at[sequence[jnp.where(places < fixed, places, shifted)]].set(jnp.asarray(lengths, jnp.int32))

    lengths = jnp.where(number % 4 == 0, named(heavy_load, number // 4), named(ordinary, number - number // 4 - 1))
    mixed = jax.random.permutation(jax.random.fold_in(own, 3), number_of)
    source_of, sink = mixed[0:number_of // 2 * 2:2], mixed[1:number_of // 2 * 2:2]
    room = jnp.minimum(lengths[source_of] - 1, limit - lengths[sink]) // 2
    room = jnp.where((source_of == sequence[0]) | (sink == sequence[0]) | (lengths[sink] == 0), 0, jnp.maximum(room, 0))
    shifted = jax.random.randint(jax.random.fold_in(own, 4), (number_of // 2,), 0, 1 << 20) % (room + 1)
    lengths = lengths.at[source_of].add(-shifted).at[sink].add(shifted)
    items = jnp.searchsorted(jnp.cumsum(lengths), jnp.arange(rows * top), side="right").astype(jnp.int32)
    listing = items.reshape(top, rows).T
    listing = listing[jax.random.permutation(jax.random.fold_in(own, 1), rows)]
    offset_by = jax.random.randint(jax.random.fold_in(own, 2), (rows, 1), 0, top)
    return jnp.take_along_axis(listing, (jnp.arange(top)[None, :] + offset_by) % top, axis=1)


def shares(amount, total, limit, lean, full):
    weights = [(1 << 20) // math.isqrt(standing ** lean) + 1 for standing in range(1, amount + 1)]
    largest = limit if full else min(limit, max(-(-total // amount), total * weights[0] // sum(weights)))
    least = 1 if total - largest >= amount - 1 else 0
    given, surplus = [largest] + [least] * (amount - 1), total - largest - least * (amount - 1)
    while surplus > 0:
        movable = [i for i in range(1, amount) if given[i] < largest] or [i for i in range(1, amount) if given[i] < limit]
        pool, left = sum([weights[i] for i in movable]), surplus
        for i in movable:
            extra = min(limit - given[i], max(1, left * weights[i] // pool), surplus)
            given[i] = given[i] + extra
            surplus = surplus - extra
    return np.array(given)


def scatter_about(own_key, extent, deviation, limit, split=(), held_as=jnp.bfloat16):
    values = jax.random.normal(own_key, extent, jnp.float32) * deviation
    if len(split) > 0:
        values = block_scale(own_key, extent, split, -0.22, 0.18) * values
    return jnp.clip(values, min=-limit, max=limit).astype(held_as)


def setup_inputs(seed: int = 0) -> dict:
    arg_keys = jax.random.split(jax.random.key(seed), 9)
    tokens = scatter_about(arg_keys[0], (TOKENS, D), 1.0, 6.0, ((0, 256),))
    grad_out = scatter_about(arg_keys[1], (TOKENS, D), 0.25, 1.5, ((0, 256),))
    routes_keys = jax.random.split(jax.random.fold_in(arg_keys[2], 1), TOKENS // TOK_DEV)
    routes_turns = jax.random.permutation(jax.random.fold_in(arg_keys[2], 3), TOKENS // TOK_DEV)
    routes = jax.vmap(lambda own, number: shared_out(jax.random.fold_in(arg_keys[2], 2), own, number, TOK_DEV, EXPERTS, TOP, CAP, 2))(routes_keys, routes_turns).reshape((TOKENS, TOP))
    gate_fixed = plant(jax.random.randint(arg_keys[3], (TOKENS, TOP), 26, 257), jax.random.fold_in(arg_keys[3], 1), 26, 256).astype(jnp.int32)
    live_count = uneven_parts(arg_keys[4], DEVICES, LIVE, TOK_DEV, 2).astype(jnp.int32)
    w_gate = scatter_about(arg_keys[5], (EXPERTS, D, FF), D ** -0.5, 0.125, ((0, 32), (1, 8)))
    w_up = scatter_about(arg_keys[6], (EXPERTS, D, FF), D ** -0.5, 0.125, ((0, 32), (1, 8)))
    w_down = scatter_about(arg_keys[7], (EXPERTS, FF, D), FF ** -0.5, 0.21875, ((0, 32), (2, 8)))
    return dict(tokens=tokens, grad_out=grad_out, routes=routes, gate_fixed=gate_fixed, live_count=live_count, w_gate=w_gate, w_up=w_up, w_down=w_down)


def contract_last(left, right):
    return lax.dot_general(left, right, (((1,), (1,)), ((), ())), preferred_element_type=jnp.float32)


def round_partials(partials):
    rounded = lax.optimization_barrier(partials.astype(jnp.bfloat16))
    return jnp.sum(rounded.astype(jnp.float32), axis=0).astype(jnp.bfloat16)


def reference(tokens, grad_out, routes, gate_fixed, live_count, w_gate, w_up, w_down):
    sources = N_DP * N_EXPERT
    per_source = TOK_DEV * TOP
    slot_rows = sources * CAP
    flat_routes = routes.reshape(sources, per_source).astype(jnp.int32)
    positions = jnp.arange(TOK_DEV, dtype=jnp.int32)
    live_tokens = positions[None, :] < live_count.astype(jnp.int32)[:, None]
    live_routes = jnp.repeat(live_tokens, TOP, axis=1)
    expert_iota = jnp.arange(EXPERTS, dtype=jnp.int32)
    matches = ((flat_routes[:, :, None] == expert_iota[None, None, :]) & live_routes[:, :, None]).astype(jnp.int32)
    slot_rank = jnp.sum((jnp.cumsum(matches, axis=1) - matches) * matches, axis=2).astype(jnp.int32)
    anchor = jnp.arange(sources, dtype=jnp.int32)[:, None]
    slot_index = jnp.where(live_routes, flat_routes * slot_rows + anchor * CAP + slot_rank, EXPERTS * slot_rows).astype(jnp.int32)
    assigned = jnp.arange(sources * per_source, dtype=jnp.int32)
    table = jnp.full((EXPERTS * slot_rows,), TOKENS * TOP, jnp.int32)
    table = table.at[slot_index.reshape(-1)].set(assigned, mode="drop").reshape(EXPERTS, slot_rows)
    gate_values = (gate_fixed.reshape(-1).astype(jnp.float32) / 256.0).astype(jnp.bfloat16)

    def per_expert(carry, inputs):
        token_sum, gate_sum = carry
        assignment, weight_gate, weight_up, weight_down = inputs
        token_index = (assignment // TOP).astype(jnp.int32)
        inputs_rows = jnp.take(tokens, token_index, axis=0, mode="fill", fill_value=0)
        grads_rows = jnp.take(grad_out, token_index, axis=0, mode="fill", fill_value=0)
        gate_scale = jnp.take(gate_values, assignment, axis=0, mode="fill", fill_value=0).astype(jnp.float32)[:, None]
        gate_pre = jnp.dot(inputs_rows, weight_gate, preferred_element_type=jnp.float32)
        up_pre = jnp.dot(inputs_rows, weight_up, preferred_element_type=jnp.float32)
        sigmoid_val = jax.nn.sigmoid(gate_pre)
        activated = gate_pre * sigmoid_val
        hidden = activated * up_pre
        back_hidden = contract_last(grads_rows, weight_down)
        route_grad = jnp.sum(back_hidden * hidden, axis=1).astype(jnp.bfloat16)
        scaled = gate_scale * back_hidden
        up_delta = (scaled * activated).astype(jnp.bfloat16)
        gate_delta = (scaled * up_pre * sigmoid_val * (1.0 + gate_pre * (1.0 - sigmoid_val))).astype(jnp.bfloat16)
        weighted = (gate_scale * hidden).astype(jnp.bfloat16)
        slot_dx = (contract_last(gate_delta, weight_gate) + contract_last(up_delta, weight_up)).astype(jnp.bfloat16)
        token_sum = token_sum.at[token_index].add(slot_dx.astype(jnp.float32), mode="drop")
        gate_sum = gate_sum.at[assignment].set(route_grad.astype(jnp.float32), mode="drop")
        inputs_parts = inputs_rows.reshape(N_DP, N_EXPERT * CAP, D).astype(jnp.float32)
        grads_parts = grads_rows.reshape(N_DP, N_EXPERT * CAP, D).astype(jnp.float32)
        gate_parts = gate_delta.reshape(N_DP, N_EXPERT * CAP, FF).astype(jnp.float32)
        up_parts = up_delta.reshape(N_DP, N_EXPERT * CAP, FF).astype(jnp.float32)
        weighted_parts = weighted.reshape(N_DP, N_EXPERT * CAP, FF).astype(jnp.float32)
        grad_gate_one = round_partials(jnp.einsum("prd,prf->pdf", inputs_parts, gate_parts))
        grad_up_one = round_partials(jnp.einsum("prd,prf->pdf", inputs_parts, up_parts))
        grad_down_one = round_partials(jnp.einsum("prf,prd->pfd", weighted_parts, grads_parts))
        return (token_sum, gate_sum), (grad_gate_one, grad_up_one, grad_down_one)

    start = (jnp.zeros((TOKENS, D), jnp.float32), jnp.zeros((TOKENS * TOP,), jnp.float32))
    (token_sum, gate_sum), (grad_gate, grad_up, grad_down) = lax.scan(per_expert, start, (table, w_gate, w_up, w_down))
    d_tokens = token_sum.astype(jnp.bfloat16)
    d_gates = gate_sum.reshape(TOKENS, TOP).astype(jnp.bfloat16)
    return d_tokens, d_gates, grad_gate, grad_up, grad_down
```

```python
import jax
import jax.numpy as jnp
from jax import lax
from jax.sharding import PartitionSpec as P

NZ, NY, NX = 8, 4, 4
ALL = ("dp", "expert")
CAP = 16
GROUP = 2 * NX


def place(index):
    dp, expert = divmod(index, (NZ // 2) * GROUP)
    z_lo, y = divmod(dp, NY)
    z_hi, rest = divmod(expert, GROUP)
    x, core = divmod(rest, 2)
    return 2 * z_hi + z_lo, y, x, core


def index_of(z, y, x, core):
    z, y, x = z % NZ, y % NY, x % NX
    return ((z % 2) * NY + y) * (NZ // 2) * GROUP + (z // 2) * GROUP + x * 2 + core


def move(array, to):
    pairs = [(i, index_of(*to(*place(i)))) for i in range(NZ * NY * GROUP)]
    return lax.ppermute(array, ALL, pairs)


def across(z, y, x, core):
    return (z + 1 if z % 2 else z - 1), y, x, core


def onward(z, y, x, core):
    return (z - 2 if z % 2 else z + 2), y, x, core


def backward(z, y, x, core):
    return (z + 2 if z % 2 else z - 2), y, x, core


def twin(z, y, x, core):
    return z ^ 1, y, x, core


def y_by(step):
    return lambda z, y, x, core: (z, y + step, x, core)


def x_by(step, flip):
    return lambda z, y, x, core: (z, y, x + step, core ^ flip)


def dot(left, right, dims):
    return lax.dot_general(left, right, (dims, ((), ())), preferred_element_type=jnp.float32)


def bf16(array):
    return array.astype(jnp.bfloat16)


def f32(array):
    return array.astype(jnp.float32)


def hold(array, *after):
    return lax.optimization_barrier((array,) + after)[0]


def local(tokens, grad_out, routes, gate_fixed, live_count, w_gate, w_up, w_down):
    rows, width = tokens.shape
    hidden_units = w_gate.shape[2]
    shard = w_gate.shape[1]
    half = shard // 2
    dp = lax.axis_index("dp")
    expert = lax.axis_index("expert")
    z_lo, y = dp // NY, dp % NY
    z_hi, x, core = expert // GROUP, (expert % GROUP) // 2, expert % 2

    live = jnp.arange(rows, dtype=jnp.int32)[None, :] < live_count[0]
    meta = jnp.concatenate([jnp.where(live, routes.T, -1), gate_fixed.T], axis=0)
    meta_near = jnp.stack([meta, move(meta, across)])
    meta_all = jnp.concatenate([meta_near, move(meta_near, onward)])

    tok_near = move(tokens, across)
    tok_far = move(tokens, onward)
    tok_last = move(tok_near, onward)
    grad_first = hold(grad_out, tok_near)
    grad_near = move(grad_first, across)
    grad_far = move(grad_first, onward)
    grad_last = move(grad_near, onward)

    own = jnp.stack([w_gate[0], w_up[0], w_down[0].T])
    other = move(own, twin)
    gathered = []
    for block in (own, other):
        from_left = move(block, y_by(1))
        from_right = move(block, y_by(-1))
        far_top = move(from_left[:, :half], y_by(1))
        far_low = move(from_right[:, half:], y_by(-1))
        gathered.append((block, from_right, (far_top, far_low), from_left))
    full = []
    for at in range(3):
        whole = jnp.zeros((2 * NY * shard, hidden_units), jnp.bfloat16)
        for far_z in range(2):
            for dy in range(NY):
                start = (((z_lo + far_z) % 2) * NY + (y + dy) % NY) * shard
                block = gathered[far_z][dy]
                if dy == 2:
                    whole = lax.dynamic_update_slice(whole, block[0][at], (start, 0))
                    whole = lax.dynamic_update_slice(whole, block[1][at], (start + half, 0))
                else:
                    whole = lax.dynamic_update_slice(whole, block[at], (start, 0))
        full.append(whole)
    full_gate, full_up, full_down = full

    destinations = [(dx, flip) for dx in range(NX) for flip in range(2)]
    wanted = jnp.stack([z_hi * GROUP + ((x + dx) % NX) * 2 + (core ^ flip) for dx, flip in destinations])
    route_a, route_b = meta_all[:, 0], meta_all[:, 1]
    hit_a = route_a[None] == wanted[:, None, None]
    hit_b = route_b[None] == wanted[:, None, None]
    hit = (hit_a | hit_b).astype(jnp.bfloat16)
    before = (jnp.arange(rows)[:, None] < jnp.arange(rows)[None, :]).astype(jnp.bfloat16)
    rank = dot(hit, before, ((2,), (0,)))
    ranks = jnp.arange(CAP, dtype=jnp.float32)[None, None, :, None]
    chosen = (rank[:, :, None, :] == ranks) & (hit[:, :, None, :] > 0)
    sources = meta_all.shape[0]
    same = jnp.eye(sources, dtype=jnp.bool_)[None, :, None, :, None]

    def spread(mask, values):
        wide = jnp.where(mask[:, :, :, None, :] & same, values, 0)
        return bf16(wide).reshape(len(destinations) * sources * CAP, sources * rows)

    gates = f32(meta_all[:, 2:]) / 256.0
    gate_of = jnp.where(hit_a, gates[None, :, 0], gates[None, :, 1])
    pick = spread(chosen, 1.0)
    pick_gate = spread(chosen, gate_of[:, :, None, None, :])
    pick_a = spread(chosen & hit_a[:, :, None, :], 1.0)
    pick_b = spread(chosen & hit_b[:, :, None, :], 1.0)

    def hand_out(picker, parts):
        sent = bf16(dot(picker, jnp.concatenate(parts), ((1,), (0,))))
        sent = sent.reshape(len(destinations), sources * CAP, width)
        return jnp.concatenate(
            [sent[k] if k == 0 else move(sent[k], x_by(*to)) for k, to in enumerate(destinations)]
        )

    in_rows = hand_out(pick, [tokens, tok_near, tok_far, tok_last])
    grad_rows = hand_out(pick_gate, [grad_out, grad_near, grad_far, grad_last])

    gate_pre = dot(in_rows, full_gate, ((1,), (0,)))
    up_pre = dot(in_rows, full_up, ((1,), (0,)))
    sig = jax.nn.sigmoid(gate_pre)
    act = gate_pre * sig
    hidden = act * up_pre
    scaled = dot(grad_rows, full_down, ((1,), (0,)))
    route_grad = jnp.sum(scaled * hidden, axis=1)
    up_delta = bf16(scaled * act)
    gate_delta = bf16(scaled * up_pre * sig * (1.0 + gate_pre * (1.0 - sig)))

    def reduce_shares(left, right):
        share = bf16(dot(left, right, ((0,), (0,)))).reshape(2, NY, shard, hidden_units)

        def towards(dy):
            return lax.dynamic_index_in_dim(share, (y + dy) % NY, 1, False)

        far = towards(2)
        top = move(far[:, :half], y_by(1))
        low = move(far[:, half:], y_by(-1))
        up_one, down_one = towards(1), towards(NY - 1)
        up_one = jnp.concatenate([bf16(f32(up_one[:, :half]) + f32(top)), up_one[:, half:]], axis=1)
        down_one = jnp.concatenate([down_one[:, :half], bf16(f32(down_one[:, half:]) + f32(low))], axis=1)
        total = f32(towards(0)) + f32(move(up_one, y_by(1))) + f32(move(down_one, y_by(-1)))
        theirs = move(bf16(lax.dynamic_index_in_dim(total, 1 - z_lo, 0, False)), twin)
        return bf16(lax.dynamic_index_in_dim(total, z_lo, 0, False) + f32(theirs))

    grad_down = reduce_shares(grad_rows, bf16(hidden)).T[None]
    slot_dx = bf16(
        dot(gate_delta, full_gate, ((1,), (1,))) + dot(up_delta, full_up, ((1,), (1,)))
    )
    grad_gate = reduce_shares(in_rows, gate_delta)[None]
    grad_up = reduce_shares(in_rows, up_delta)[None]

    extra = 128
    slot_back = jnp.concatenate(
        [slot_dx, jnp.broadcast_to(bf16(route_grad)[:, None], (slot_dx.shape[0], extra))], axis=1
    ).reshape(len(destinations), sources * CAP, width + extra)
    back = jnp.concatenate(
        [
            slot_back[k] if k == 0 else move(slot_back[k], x_by(-dx, flip))
            for k, (dx, flip) in enumerate(destinations)
        ]
    )
    lane = jnp.arange(extra)[None, :]
    back_dx = bf16(dot(pick, back[:, :width], ((0,), (0,))))
    back_a = dot(pick_a, back[:, width:], ((0,), (0,)))
    back_b = dot(pick_b, back[:, width:], ((0,), (0,)))
    back_gate = bf16(jnp.where(lane == 0, back_a, back_b))
    parts = jnp.concatenate([back_dx, back_gate], axis=1).reshape(sources, rows, width + extra)
    for_last = move(parts[3], backward)
    for_far = move(parts[2], backward)
    near = move(bf16(f32(parts[1]) + f32(for_last)), across)
    whole = f32(parts[0]) + f32(for_far) + f32(near)
    d_tokens = bf16(whole[:, :width])
    own_gate = f32(gate_fixed) / 256.0
    d_gates = bf16(whole[:, width : width + 2] / own_gate)
    return d_tokens, d_gates, grad_gate, grad_up, grad_down


def solution(mesh):
    rows = P(("dp", "expert"), None)
    return jax.shard_map(
        local,
        mesh=mesh,
        in_specs=(
            rows,
            rows,
            rows,
            rows,
            P(("dp", "expert")),
            P("expert", "dp", None),
            P("expert", "dp", None),
            P("expert", None, "dp"),
        ),
        out_specs=(
            rows,
            rows,
            P("expert", "dp", None),
            P("expert", "dp", None),
            P("expert", None, "dp"),
        ),
        check_vma=False,
    )
```

```python
import jax
import jax.numpy as jnp
from jax import lax
from jax.experimental import pallas as pl
from jax.experimental.pallas import tpu as pltpu
from jax.sharding import PartitionSpec as P

NZ, NY, NX = 8, 4, 4
ALL = ("dp", "expert")
CAP = 16
GROUP = 2 * NX


def place(index):
    dp, expert = divmod(index, (NZ // 2) * GROUP)
    z_lo, y = divmod(dp, NY)
    z_hi, rest = divmod(expert, GROUP)
    x, core = divmod(rest, 2)
    return 2 * z_hi + z_lo, y, x, core


def index_of(z, y, x, core):
    z, y, x = z % NZ, y % NY, x % NX
    return ((z % 2) * NY + y) * (NZ // 2) * GROUP + (z // 2) * GROUP + x * 2 + core


def move(array, to):
    pairs = [(i, index_of(*to(*place(i)))) for i in range(NZ * NY * GROUP)]
    return lax.ppermute(array, ALL, pairs)


def across(z, y, x, core):
    return (z + 1 if z % 2 else z - 1), y, x, core


def onward(z, y, x, core):
    return (z - 2 if z % 2 else z + 2), y, x, core


def beyond(z, y, x, core):
    return onward(*across(z, y, x, core))


def backward(z, y, x, core):
    return (z + 2 if z % 2 else z - 2), y, x, core


def twin(z, y, x, core):
    return z ^ 1, y, x, core


def y_by(step):
    return lambda z, y, x, core: (z, y + step, x, core)


def dot(left, right, dims):
    return lax.dot_general(left, right, (dims, ((), ())), preferred_element_type=jnp.float32)


def bf16(array):
    return array.astype(jnp.bfloat16)


def f32(array):
    return array.astype(jnp.float32)


def hold(array, *after):
    return lax.optimization_barrier((array,) + after)[0]


ORDER = [(dy, far, low) for far in (1, 0) for dy in (2, 1, 3, 0) for low in (0, 1)]


def pieces(array, starts, size):
    return jnp.concatenate([lax.dynamic_slice_in_dim(array, at, size, 1) for at in starts], axis=1)


def reorder(array, order, size, base=0):
    parts = [array[..., base + at * size : base + (at + 1) * size] for at in order]
    return jnp.concatenate(parts, axis=-1)


def turn(place_ref, tok_ref, grad_ref, out_ref):
    z_lo, y = place_ref[0], place_ref[1]
    half = out_ref.shape[2] // len(ORDER)
    for n, (dy, far, low) in enumerate(ORDER):
        at = (((z_lo + far) & 1) * NY + ((y + dy) & (NY - 1))) * 2 + low
        at = pl.multiple_of(at * half, half)
        out_ref[0, :, n * half : (n + 1) * half] = tok_ref[:, pl.ds(at, half)]
        out_ref[1, :, n * half : (n + 1) * half] = grad_ref[:, pl.ds(at, half)]


def gather_near(own_ref, other_ref, tok_ref, grad_ref):
    rows, width = own_ref.shape[1:]
    for n, out_ref in enumerate((tok_ref, grad_ref)):
        out_ref[:rows] = own_ref[n]
        out_ref[rows:, : width // 2] = other_ref[n, :, width // 2 :]
        out_ref[rows:, width // 2 :] = other_ref[n, :, : width // 2]


def to_slots(*refs):
    out_ref = refs[-1]
    count, base = out_ref.shape[0], 0
    for pick_ref, rows_ref in zip(refs[:-1:2], refs[1:-1:2]):
        found = jnp.dot(pick_ref[...], rows_ref[...], preferred_element_type=jnp.float32)
        found = found.astype(jnp.bfloat16).reshape(count, -1, found.shape[1])
        out_ref[:, base : base + found.shape[1], :] = found
        base += found.shape[1]


def on_core(body, shapes, *arrays):
    in_vmem = pl.BlockSpec(memory_space=pltpu.VMEM)
    return pl.pallas_call(
        body,
        out_shape=shapes,
        in_specs=[in_vmem] * len(arrays),
        out_specs=jax.tree.map(lambda _: in_vmem, shapes),
        compiler_params=pltpu.CompilerParams(vmem_limit_bytes=32 << 20),
        cost_estimate=pl.CostEstimate(flops=0, bytes_accessed=0, transcendentals=0),
    )(*arrays)


def local(tokens, grad_out, routes, gate_fixed, live_count, w_gate, w_up, w_down):
    rows, width = tokens.shape
    hidden_units = w_gate.shape[2]
    shard = w_gate.shape[1]
    half = shard // 2
    dp = lax.axis_index("dp")
    expert = lax.axis_index("expert")
    z_lo, y = dp // NY, dp % NY
    z_hi = expert // GROUP

    in_vmem = pl.BlockSpec(memory_space=pltpu.VMEM)
    both = pl.pallas_call(
        turn,
        out_shape=jax.ShapeDtypeStruct((2, rows, width), jnp.bfloat16),
        in_specs=[pl.BlockSpec(memory_space=pltpu.SMEM), in_vmem, in_vmem],
        out_specs=in_vmem,
        cost_estimate=pl.CostEstimate(flops=0, bytes_accessed=0, transcendentals=0),
    )(jnp.stack([z_lo, y]).astype(jnp.int32), tokens, grad_out)

    def swap_halves(array):
        return jnp.concatenate([array[..., width // 2 : width], array[..., : width // 2], array[..., width:]], axis=-1)

    live = jnp.arange(rows, dtype=jnp.int32)[None, :] < live_count[0]
    meta = jnp.concatenate([jnp.where(live, routes.T, -1), gate_fixed.T], axis=0)
    meta_all = jnp.stack([meta, move(meta, across), move(meta, onward), move(meta, beyond)])

    both = hold(both, meta_all)
    both_across = move(both, across)
    w_gate = hold(w_gate, both)
    own = jnp.concatenate([w_gate[0], w_up[0], w_down[0].T], axis=1)
    own_left, own_right = move(own, y_by(1)), move(own, y_by(-1))
    twins = move(own, twin)
    wide = jax.ShapeDtypeStruct((2 * rows, width), jnp.bfloat16)
    tok_near, grad_near = on_core(gather_near, (wide, wide), both, both_across)
    tok_far = move(tok_near, onward)
    twins = hold(twins, own_left, own_right)
    twin_left, twin_right = move(twins, y_by(1)), move(twins, y_by(-1))
    grad_far = move(hold(grad_near, tok_far), onward)

    wanted = z_hi * GROUP + jnp.arange(GROUP, dtype=jnp.int32)
    route_a, route_b = meta_all[:, 0], meta_all[:, 1]
    hit_a = route_a[None] == wanted[:, None, None]
    hit_b = route_b[None] == wanted[:, None, None]
    hit = (hit_a | hit_b).astype(jnp.bfloat16)
    before = (jnp.arange(rows)[:, None] < jnp.arange(rows)[None, :]).astype(jnp.bfloat16)
    rank = dot(hit, before, ((2,), (0,)))
    ranks = jnp.arange(CAP, dtype=jnp.float32)[None, None, :, None]
    chosen = (rank[:, :, None, :] == ranks) & (hit[:, :, None, :] > 0)
    gates = f32(meta_all[:, 2:]) / 256.0
    gate_of = jnp.where(hit_a, gates[None, :, 0], gates[None, :, 1])[:, :, None, :]
    ones = jnp.where(chosen, 1.0, 0.0)
    scales = jnp.where(chosen, gate_of, 0.0)
    slots = GROUP * 2 * CAP

    def spread(maps):
        n = maps.shape[1]
        same = jnp.eye(n, dtype=jnp.bool_)[None, :, None, :, None]
        return bf16(jnp.where(same, maps[:, :, :, None, :], 0.0)).reshape(GROUP * n * CAP, n * rows)

    pick_near, pick_far = spread(ones[:, :2]), spread(ones[:, 2:])
    pick_gate_near, pick_gate_far = spread(scales[:, :2]), spread(scales[:, 2:])
    groups = [list(range(h * GROUP, (h + 1) * GROUP)) for h in range(NZ // 2)]

    def exchange(array):
        return lax.all_to_all(
            array.reshape(GROUP, -1, array.shape[1]), "expert", 0, 0, axis_index_groups=groups, tiled=True
        )

    def slots_of(*pairs):
        shape = jax.ShapeDtypeStruct((GROUP, len(pairs) // 2 * 2 * CAP, width), jnp.bfloat16)
        return on_core(to_slots, shape, *pairs)

    pick_now = hold(pick_near, pick_far, pick_gate_far)
    near_sent = slots_of(pick_now, tok_near, pick_gate_near, grad_near)
    near_rows = exchange(near_sent.reshape(2 * slots, width))
    tok_sent = slots_of(pick_far, tok_far)
    in_rows = jnp.concatenate(
        [near_rows[:, : 2 * CAP].reshape(slots, width), exchange(tok_sent.reshape(slots, width)).reshape(slots, width)]
    )
    grad_sent = slots_of(pick_gate_far, grad_far)
    grad_rows = jnp.concatenate(
        [near_rows[:, 2 * CAP :].reshape(slots, width), exchange(grad_sent.reshape(slots, width)).reshape(slots, width)]
    )

    top_own, low_own = (move(hold(part, near_sent), y_by(step)) for part, step in ((own_left[:half], 1), (own_right[half:], -1)))
    top_twin, low_twin = (move(hold(part, tok_sent), y_by(step)) for part, step in ((twin_left[:half], 1), (twin_right[half:], -1)))
    top_twin, low_twin = hold(top_twin, grad_sent), hold(low_twin, grad_sent)
    full = jnp.concatenate(
        [top_twin, low_twin, twin_right, twin_left, twins, top_own, low_own, own_right, own_left, own]
    )
    pre = dot(in_rows, full[:, : 2 * hidden_units], ((1,), (0,)))
    gate_pre, up_pre = pre[:, :hidden_units], pre[:, hidden_units:]
    sig = jax.nn.sigmoid(gate_pre)
    act = gate_pre * sig
    hidden = act * up_pre
    weighted = bf16(hidden)
    slope = up_pre * sig * (1.0 + gate_pre * (1.0 - sig))

    def share(left, right, first, count):
        return bf16(dot(left[:, first * half : (first + count) * half], right, ((0,), (0,))))

    down_theirs = share(grad_rows, weighted, 0, 8)
    scaled = dot(hold(grad_rows, down_theirs), full[:, 2 * hidden_units :], ((1,), (0,)))
    down_theirs = move(down_theirs, twin)
    route_grad = jnp.sum(scaled * hidden, axis=1)
    deltas = bf16(jnp.concatenate([scaled * slope, scaled * act], axis=1))
    middle = width // 2
    ends = [
        jnp.concatenate([in_rows[:, at : at + half], in_rows[:, middle + at : middle + at + half]], axis=1)
        for at in (0, half)
    ]
    top, low = (share(part, deltas, 0, 2) for part in ends)
    ready = hold(deltas, top, low)
    top, low = move(top, y_by(1)), move(low, y_by(-1))

    extra = 128
    lane = jnp.arange(extra, dtype=jnp.int32)[None, :]
    tail = bf16(jnp.where(lane == expert, route_grad[:, None], 0.0))

    def row_grads(delta, at):
        slot_dx = bf16(dot(delta, full[:, : 2 * hidden_units], ((1,), (1,))))
        return jnp.concatenate([slot_dx, tail[at : at + slots]], axis=1)

    dx_far = row_grads(ready[slots:], slots)
    back_far = exchange(dx_far).reshape(slots, width + extra)
    dx_near = row_grads(hold(ready[:slots], dx_far), 0)
    back_near = exchange(dx_near).reshape(slots, width + extra)

    def around(top, low, up, down, stay):
        up = jnp.concatenate([bf16(f32(up[:half]) + f32(top)), up[half:]])
        down = jnp.concatenate([down[:half], bf16(f32(down[half:]) + f32(low))])
        return f32(stay) + f32(move(up, y_by(1))) + f32(move(down, y_by(-1)))

    left = hold(in_rows, dx_near)
    theirs = bf16(around(top[:half], low[:half], *(share(left, deltas, at, 2) for at in (2, 4, 6))))
    down_sum = bf16(f32(share(hold(grad_rows, dx_near), weighted, 8, 8)) + f32(down_theirs))
    down_top, down_low = move(down_sum[:half], y_by(1)), move(down_sum[half:shard], y_by(-1))
    top = hold(top, theirs)
    theirs = move(theirs, twin)
    mine = around(top[half:], low[half:], *(share(left, deltas, at, 2) for at in (10, 12, 14)))
    total = around(down_top, down_low, *(down_sum[n * shard : (n + 1) * shard] for n in (1, 2, 3)))
    grad_down = bf16(total).T[None]
    total = bf16(mine + f32(theirs))
    grad_gate, grad_up = total[None, :, :hidden_units], total[None, :, hidden_units:]

    parts_far = bf16(dot(pick_far, back_far, ((0,), (0,))))
    for_near = f32(move(parts_far, backward))
    parts_near = dot(pick_near, back_near, ((0,), (0,)))
    for_across = move(bf16(swap_halves(parts_near[rows:] + for_near[rows:])), across)
    whole = parts_near[:rows] + for_near[:rows] + f32(for_across)
    plain = [ORDER.index((dy, far, low)) for far in range(2) for dy in range(NY) for low in range(2)]
    ordered = reorder(bf16(whole[:, :width]), plain, half)
    spots = [((z + z_lo) % 2 * NY + (at - y) % NY) * shard for z in range(2) for at in range(NY)]
    d_tokens = pieces(ordered, spots, shard)
    found = jnp.where(lane[:, None, :] == routes[:, :, None], whole[:, None, width:], 0.0)
    d_gates = bf16(jnp.sum(found, axis=2) / (f32(gate_fixed) / 256.0))
    return d_tokens, d_gates, grad_gate, grad_up, grad_down


def solution(mesh):
    rows = P(("dp", "expert"), None)
    return jax.shard_map(
        local,
        mesh=mesh,
        in_specs=(
            rows,
            rows,
            rows,
            rows,
            P(("dp", "expert")),
            P("expert", "dp", None),
            P("expert", "dp", None),
            P("expert", None, "dp"),
        ),
        out_specs=(
            rows,
            rows,
            P("expert", "dp", None),
            P("expert", "dp", None),
            P("expert", None, "dp"),
        ),
        check_vma=False,
    )
```

```python
import jax
import jax.numpy as jnp
from jax import lax
from jax.experimental import pallas as pl
from jax.experimental.pallas import tpu as pltpu
from jax.sharding import PartitionSpec as P

NZ, NY, NX = 8, 4, 4
ALL = ("dp", "expert")
CAP = 16
CODES = 16
GROUP = 2 * NX


def place(index):
    dp, expert = divmod(index, (NZ // 2) * GROUP)
    z_lo, y = divmod(dp, NY)
    z_hi, rest = divmod(expert, GROUP)
    x, core = divmod(rest, 2)
    return 2 * z_hi + z_lo, y, x, core


def index_of(z, y, x, core):
    z, y, x = z % NZ, y % NY, x % NX
    return ((z % 2) * NY + y) * (NZ // 2) * GROUP + (z // 2) * GROUP + x * 2 + core


def move(array, to):
    pairs = [(i, index_of(*to(*place(i)))) for i in range(NZ * NY * GROUP)]
    return lax.ppermute(array, ALL, pairs)


def across(z, y, x, core):
    return (z + 1 if z % 2 else z - 1), y, x, core


def onward(z, y, x, core):
    return (z - 2 if z % 2 else z + 2), y, x, core


def beyond(z, y, x, core):
    return onward(*across(z, y, x, core))


def backward(z, y, x, core):
    return (z + 2 if z % 2 else z - 2), y, x, core


def twin(z, y, x, core):
    return z ^ 1, y, x, core


def y_by(step):
    return lambda z, y, x, core: (z, y + step, x, core)


def dot(left, right, dims):
    return lax.dot_general(left, right, (dims, ((), ())), preferred_element_type=jnp.float32)


def bf16(array):
    return array.astype(jnp.bfloat16)


def f32(array):
    return array.astype(jnp.float32)


def hold(array, *after):
    return lax.optimization_barrier((array,) + after)[0]


ORDER = [(dy, far, low) for far in (1, 0) for dy in (2, 1, 3, 0) for low in (0, 1)]


def pieces(array, starts, size):
    return jnp.concatenate([lax.dynamic_slice_in_dim(array, at, size, 1) for at in starts], axis=1)


def reorder(array, order, size, base=0):
    parts = [array[..., base + at * size : base + (at + 1) * size] for at in order]
    return jnp.concatenate(parts, axis=-1)


def turn(place_ref, codes_ref, tok_ref, grad_ref, out_ref):
    z_lo, y, live = place_ref[0], place_ref[1], place_ref[2]
    rows, width = tok_ref.shape
    half = width // len(ORDER)
    for n, (dy, far, low) in enumerate(ORDER):
        at = (((z_lo + far) & 1) * NY + ((y + dy) & (NY - 1))) * 2 + low
        at = pl.multiple_of(at * half, half)
        out_ref[:rows, n * half : (n + 1) * half] = tok_ref[:, pl.ds(at, half)]
        out_ref[rows : 2 * rows, n * half : (n + 1) * half] = grad_ref[:, pl.ds(at, half)]
    out_ref[2 * rows :] = jnp.zeros((CODES, width), jnp.bfloat16)
    row = lax.broadcasted_iota(jnp.int32, codes_ref.shape, 0)
    dead = ((row & 3) < 2) & (lax.broadcasted_iota(jnp.int32, codes_ref.shape, 1) >= live)
    out_ref[2 * rows :, :rows] = jnp.where(dead, -1, codes_ref[...]).astype(jnp.float32).astype(jnp.bfloat16)


def gather_near(own_ref, other_ref, tok_ref, grad_ref):
    width = own_ref.shape[1]
    middle = width // 2
    rows = grad_ref.shape[0] // 2
    for at, out_ref in ((0, tok_ref), (rows, grad_ref)):
        out_ref[:rows] = own_ref[at : at + rows]
        out_ref[rows : 2 * rows, :middle] = other_ref[at : at + rows, middle:]
        out_ref[rows : 2 * rows, middle:] = other_ref[at : at + rows, :middle]
    own, other = own_ref[2 * rows :, :rows].astype(jnp.float32), other_ref[2 * rows :, :rows].astype(jnp.float32)
    first = lax.broadcasted_iota(jnp.int32, own.shape, 0) < 4
    tok_ref[2 * rows :] = jnp.zeros((CODES, width), jnp.bfloat16)
    tok_ref[2 * rows :, :rows] = jnp.where(first, own, other).astype(jnp.bfloat16)


def slot_maps(base_ref, codes_ref, pick_ref, gate_ref):
    rows = pick_ref.shape[1] // 2
    codes = codes_ref[:, :rows].astype(jnp.float32)
    wanted = (lax.broadcasted_iota(jnp.int32, (GROUP, rows), 0) + base_ref[0]).astype(jnp.float32)
    at = lax.broadcasted_iota(jnp.int32, (rows, rows), 0)
    before = (at < lax.broadcasted_iota(jnp.int32, (rows, rows), 1)).astype(jnp.float32).astype(jnp.bfloat16)
    order = lax.broadcasted_iota(jnp.int32, (CAP, rows), 0).astype(jnp.float32)
    nothing = jnp.zeros((CAP, rows), jnp.bfloat16)
    for n in range(2):
        route_a, route_b, gate_a, gate_b = (codes[4 * n + k : 4 * n + k + 1] for k in range(4))
        hit_a, hit_b = wanted == route_a, wanted == route_b
        hit = jnp.where(hit_a | hit_b, 1.0, 0.0)
        rank = jnp.dot(hit.astype(jnp.bfloat16), before, preferred_element_type=jnp.float32)
        rank = jnp.where(hit > 0, rank, -1.0)
        gate = jnp.where(hit_a, gate_a, gate_b) * (1.0 / 256.0)
        for to in range(GROUP):
            held = order == rank[to : to + 1]
            slots = slice((to * 2 + n) * CAP, (to * 2 + n + 1) * CAP)
            here, there = slice(n * rows, (n + 1) * rows), slice((1 - n) * rows, (2 - n) * rows)
            pick_ref[slots, here] = jnp.where(held, 1.0, 0.0).astype(jnp.bfloat16)
            gate_ref[slots, here] = jnp.where(held, gate[to : to + 1], 0.0).astype(jnp.bfloat16)
            pick_ref[slots, there] = nothing
            gate_ref[slots, there] = nothing


def cut(own_left, twin_left, own_right, twin_right, top_ref, low_ref):
    half = top_ref.shape[0] // 2
    top_ref[:half] = own_left[:half]
    top_ref[half:] = twin_left[:half]
    low_ref[:half] = own_right[half:]
    low_ref[half:] = twin_right[half:]


def to_slots(*refs):
    out_ref = refs[-1]
    count, base = out_ref.shape[0], 0
    for pick_ref, rows_ref in zip(refs[:-1:2], refs[1:-1:2]):
        rows = rows_ref[: pick_ref.shape[1]]
        found = jnp.dot(pick_ref[...], rows, preferred_element_type=jnp.float32)
        found = found.astype(jnp.bfloat16).reshape(count, -1, found.shape[1])
        out_ref[:, base : base + found.shape[1], :] = found
        base += found.shape[1]


def on_core(body, shapes, *arrays, us=0, scalars=0):
    in_vmem = pl.BlockSpec(memory_space=pltpu.VMEM)
    return pl.pallas_call(
        body,
        out_shape=shapes,
        in_specs=[pl.BlockSpec(memory_space=pltpu.SMEM)] * scalars + [in_vmem] * (len(arrays) - scalars),
        out_specs=jax.tree.map(lambda _: in_vmem, shapes),
        compiler_params=pltpu.CompilerParams(vmem_limit_bytes=32 << 20),
        cost_estimate=pl.CostEstimate(flops=us * 1_000_000_000, bytes_accessed=us * 3_300_000, transcendentals=us * 1_000_000),
    )(*arrays)


def keep(in_ref, out_ref):
    out_ref[...] = in_ref[...]


def pace(small, *after):
    return on_core(keep, jax.ShapeDtypeStruct(small.shape, small.dtype), hold(small, *after), us=100)


def local(tokens, grad_out, routes, gate_fixed, live_count, w_gate, w_up, w_down):
    rows, width = tokens.shape
    hidden_units = w_gate.shape[2]
    shard = w_gate.shape[1]
    half = shard // 2
    dp = lax.axis_index("dp")
    expert = lax.axis_index("expert")
    z_lo, y = dp // NY, dp % NY
    z_hi = expert // GROUP

    def bf16_type(*shape):
        return jax.ShapeDtypeStruct(shape, jnp.bfloat16)

    codes = jnp.tile(jnp.concatenate([routes.T, gate_fixed.T]), (CODES // 4, 1))
    place_now = jnp.stack([z_lo, y, live_count[0]]).astype(jnp.int32)
    both = on_core(turn, bf16_type(2 * rows + CODES, width), place_now, codes, tokens, grad_out, scalars=1)

    def swap_halves(array):
        return jnp.concatenate([array[..., width // 2 : width], array[..., : width // 2], array[..., width:]], axis=-1)

    both_across = move(both, across)
    w_gate = hold(w_gate, both)
    own = jnp.concatenate([w_gate[0], w_up[0], w_down[0].T], axis=1)
    own_left, own_right = move(own, y_by(1)), move(own, y_by(-1))
    twins = move(own, twin)
    near_types = bf16_type(2 * rows + CODES, width), bf16_type(2 * rows, width)
    tok_near, grad_near = on_core(gather_near, near_types, both, both_across)
    tok_far = move(tok_near, onward)
    twins = hold(twins, own_left, own_right)
    twin_left, twin_right = move(twins, y_by(1)), move(twins, y_by(-1))
    grad_far = move(hold(grad_near, tok_far), onward)

    slots = GROUP * 2 * CAP
    base = (z_hi * GROUP).astype(jnp.int32)[None]

    def maps(held):
        return on_core(slot_maps, (bf16_type(slots, 2 * rows),) * 2, base, held[2 * rows :], scalars=1)

    pick_near, pick_gate_near = maps(tok_near)
    pick_far, pick_gate_far = maps(tok_far)
    groups = [list(range(h * GROUP, (h + 1) * GROUP)) for h in range(NZ // 2)]

    def exchange(array):
        return lax.all_to_all(
            array.reshape(GROUP, -1, array.shape[1]), "expert", 0, 0, axis_index_groups=groups, tiled=True
        )

    def slots_of(*pairs, us=0):
        shape = jax.ShapeDtypeStruct((GROUP, len(pairs) // 2 * 2 * CAP, width), jnp.bfloat16)
        return on_core(to_slots, shape, *pairs, us=us)

    cut_type = jax.ShapeDtypeStruct((shard, 3 * hidden_units), jnp.bfloat16)
    top, low = on_core(cut, (cut_type, cut_type), own_left, twin_left, own_right, twin_right)

    pick_now = hold(pick_near, own_left, own_right, twins)
    near_sent = slots_of(pick_now, tok_near, pick_gate_near, grad_near)
    near_rows = exchange(near_sent.reshape(2 * slots, width))
    tok_sent = hold(slots_of(hold(pick_far, top, low), tok_far, us=100), near_rows)
    far_top, far_low = move(top, y_by(1)), move(low, y_by(-1))
    tok_rows = exchange(tok_sent.reshape(slots, width)).reshape(slots, width)
    grad_sent = hold(slots_of(hold(pick_gate_far, far_top, far_low), grad_far, us=100), tok_rows)
    far_rows = exchange(grad_sent.reshape(slots, width)).reshape(slots, width)
    near_later = hold(near_rows, grad_sent)
    in_rows = jnp.concatenate([near_later[:, : 2 * CAP].reshape(slots, width), tok_rows])
    grad_rows = jnp.concatenate([near_later[:, 2 * CAP :].reshape(slots, width), far_rows])
    far_top, far_low = hold(far_top, grad_sent), hold(far_low, grad_sent)
    full = jnp.concatenate(
        [far_top[half:], far_low[half:], twin_right, twin_left, twins]
        + [far_top[:half], far_low[:half], own_right, own_left, own]
    )
    pre = dot(in_rows, full[:, : 2 * hidden_units], ((1,), (0,)))
    gate_pre, up_pre = pre[:, :hidden_units], pre[:, hidden_units:]
    sig = jax.nn.sigmoid(gate_pre)
    act = gate_pre * sig
    hidden = act * up_pre
    weighted = bf16(hidden)
    slope = up_pre * sig * (1.0 + gate_pre * (1.0 - sig))

    def share(left, right, first, count):
        return bf16(dot(left[:, first * half : (first + count) * half], right, ((0,), (0,))))

    down_theirs = share(grad_rows, weighted, 0, 8)
    scaled = dot(hold(grad_rows, down_theirs), full[:, 2 * hidden_units :], ((1,), (0,)))
    down_theirs = move(down_theirs, twin)
    route_grad = jnp.sum(scaled * hidden, axis=1)
    deltas = bf16(jnp.concatenate([scaled * slope, scaled * act], axis=1))
    middle = width // 2
    ends = [
        jnp.concatenate([in_rows[:, at : at + half], in_rows[:, middle + at : middle + at + half]], axis=1)
        for at in (0, half)
    ]
    top, low = (share(part, deltas, 0, 2) for part in ends)
    ready = hold(deltas, top, low)
    top, low = move(top, y_by(1)), move(low, y_by(-1))

    extra = 128
    lane = jnp.arange(extra, dtype=jnp.int32)[None, :]
    tail = bf16(jnp.where(lane == expert, route_grad[:, None], 0.0))

    def row_grads(delta, at):
        slot_dx = bf16(dot(delta, full[:, : 2 * hidden_units], ((1,), (1,))))
        return jnp.concatenate([slot_dx, tail[at : at + slots]], axis=1)

    dx_far = row_grads(ready[slots:], slots)
    back_far = exchange(dx_far).reshape(slots, width + extra)
    gone = pace(lane + expert, top, low)
    parts_far = bf16(dot(hold(pick_far, gone), back_far, ((0,), (0,))))
    for_near = move(parts_far, backward)
    dx_near = row_grads(hold(ready[:slots], dx_far), 0)
    back_near = exchange(hold(dx_near, parts_far)).reshape(slots, width + extra)

    def around(top, low, up, down, stay):
        up = jnp.concatenate([bf16(f32(up[:half]) + f32(top)), up[half:]])
        down = jnp.concatenate([down[:half], bf16(f32(down[half:]) + f32(low))])
        return f32(stay) + f32(move(up, y_by(1))) + f32(move(down, y_by(-1)))

    gone = pace(lane + expert, for_near)
    parts_near = dot(hold(pick_near, gone), back_near, ((0,), (0,)))
    for_near = f32(for_near)
    for_across = bf16(swap_halves(parts_near[rows:] + for_near[rows:]))
    left = hold(in_rows, top, low)
    theirs = bf16(around(top[:half], low[:half], *(share(left, deltas, at, 2) for at in (2, 4, 6))))
    down_sum = bf16(f32(share(hold(grad_rows, top, low), weighted, 8, 8)) + f32(down_theirs))
    down_top, down_low = move(down_sum[:half], y_by(1)), move(down_sum[half:shard], y_by(-1))
    down_top, down_low = hold(down_top, for_across), hold(down_low, for_across)
    top, low = hold(top, theirs), hold(low, theirs)
    theirs = move(theirs, twin)
    mine = around(top[half:], low[half:], *(share(left, deltas, at, 2) for at in (10, 12, 14)))
    total = around(down_top, down_low, *(down_sum[n * shard : (n + 1) * shard] for n in (1, 2, 3)))
    grad_down = bf16(total).T[None]
    total = bf16(mine + f32(theirs))
    grad_gate, grad_up = total[None, :, :hidden_units], total[None, :, hidden_units:]

    for_across = move(for_across, across)
    whole = parts_near[:rows] + for_near[:rows] + f32(for_across)
    plain = [ORDER.index((dy, far, low)) for far in range(2) for dy in range(NY) for low in range(2)]
    ordered = reorder(bf16(whole[:, :width]), plain, half)
    spots = [((z + z_lo) % 2 * NY + (at - y) % NY) * shard for z in range(2) for at in range(NY)]
    d_tokens = pieces(ordered, spots, shard)
    found = jnp.where(lane[:, None, :] == routes[:, :, None], whole[:, None, width:], 0.0)
    d_gates = bf16(jnp.sum(found, axis=2) / (f32(gate_fixed) / 256.0))
    return d_tokens, d_gates, grad_gate, grad_up, grad_down


def solution(mesh):
    rows = P(("dp", "expert"), None)
    return jax.shard_map(
        local,
        mesh=mesh,
        in_specs=(
            rows,
            rows,
            rows,
            rows,
            P(("dp", "expert")),
            P("expert", "dp", None),
            P("expert", "dp", None),
            P("expert", None, "dp"),
        ),
        out_specs=(
            rows,
            rows,
            P("expert", "dp", None),
            P("expert", "dp", None),
            P("expert", None, "dp"),
        ),
        check_vma=False,
    )
```

```python
import jax
import jax.numpy as jnp
from jax import lax
from jax.experimental import pallas as pl
from jax.experimental.pallas import tpu as pltpu
from jax.sharding import PartitionSpec as P

NZ, NY, NX = 8, 4, 4
ALL = ("dp", "expert")
CAP = 16
CODES = 16
GROUP = 2 * NX


def place(index):
    dp, expert = divmod(index, (NZ // 2) * GROUP)
    z_lo, y = divmod(dp, NY)
    z_hi, rest = divmod(expert, GROUP)
    x, core = divmod(rest, 2)
    return 2 * z_hi + z_lo, y, x, core


def index_of(z, y, x, core):
    z, y, x = z % NZ, y % NY, x % NX
    return ((z % 2) * NY + y) * (NZ // 2) * GROUP + (z // 2) * GROUP + x * 2 + core


def move(array, to):
    pairs = [(i, index_of(*to(*place(i)))) for i in range(NZ * NY * GROUP)]
    return lax.ppermute(array, ALL, pairs)


def across(z, y, x, core):
    return (z + 1 if z % 2 else z - 1), y, x, core


def onward(z, y, x, core):
    return (z - 2 if z % 2 else z + 2), y, x, core


def beyond(z, y, x, core):
    return onward(*across(z, y, x, core))


def backward(z, y, x, core):
    return (z + 2 if z % 2 else z - 2), y, x, core


def twin(z, y, x, core):
    return z ^ 1, y, x, core


def y_by(step):
    return lambda z, y, x, core: (z, y + step, x, core)


def dot(left, right, dims):
    return lax.dot_general(left, right, (dims, ((), ())), preferred_element_type=jnp.float32)


def bf16(array):
    return array.astype(jnp.bfloat16)


def f32(array):
    return array.astype(jnp.float32)


def hold(array, *after):
    return lax.optimization_barrier((array,) + after)[0]


ORDER = [(dy, far, low) for far in (1, 0) for dy in (2, 1, 3, 0) for low in (0, 1)]


def pieces(array, starts, size):
    return jnp.concatenate([lax.dynamic_slice_in_dim(array, at, size, 1) for at in starts], axis=1)


def reorder(array, order, size, base=0):
    parts = [array[..., base + at * size : base + (at + 1) * size] for at in order]
    return jnp.concatenate(parts, axis=-1)


def turn(place_ref, codes_ref, tok_ref, grad_ref, out_ref):
    z_lo, y, live = place_ref[0], place_ref[1], place_ref[2]
    rows, width = tok_ref.shape
    half = width // len(ORDER)
    for n, (dy, far, low) in enumerate(ORDER):
        at = (((z_lo + far) & 1) * NY + ((y + dy) & (NY - 1))) * 2 + low
        at = pl.multiple_of(at * half, half)
        out_ref[:rows, n * half : (n + 1) * half] = tok_ref[:, pl.ds(at, half)]
        out_ref[rows : 2 * rows, n * half : (n + 1) * half] = grad_ref[:, pl.ds(at, half)]
    out_ref[2 * rows :] = jnp.zeros((CODES, width), jnp.bfloat16)
    row = lax.broadcasted_iota(jnp.int32, codes_ref.shape, 0)
    dead = ((row & 3) < 2) & (lax.broadcasted_iota(jnp.int32, codes_ref.shape, 1) >= live)
    out_ref[2 * rows :, :rows] = jnp.where(dead, -1, codes_ref[...]).astype(jnp.float32).astype(jnp.bfloat16)


def gather_near(own_ref, other_ref, tok_ref, grad_ref):
    width = own_ref.shape[1]
    middle = width // 2
    rows = grad_ref.shape[0] // 2
    for at, out_ref in ((0, tok_ref), (rows, grad_ref)):
        out_ref[:rows] = own_ref[at : at + rows]
        out_ref[rows : 2 * rows, :middle] = other_ref[at : at + rows, middle:]
        out_ref[rows : 2 * rows, middle:] = other_ref[at : at + rows, :middle]
    own, other = own_ref[2 * rows :, :rows].astype(jnp.float32), other_ref[2 * rows :, :rows].astype(jnp.float32)
    first = lax.broadcasted_iota(jnp.int32, own.shape, 0) < 4
    tok_ref[2 * rows :] = jnp.zeros((CODES, width), jnp.bfloat16)
    tok_ref[2 * rows :, :rows] = jnp.where(first, own, other).astype(jnp.bfloat16)


def slot_maps(base_ref, codes_ref, pick_ref, gate_ref):
    rows = pick_ref.shape[1] // 2
    codes = codes_ref[:, :rows].astype(jnp.float32)
    wanted = (lax.broadcasted_iota(jnp.int32, (GROUP, rows), 0) + base_ref[0]).astype(jnp.float32)
    at = lax.broadcasted_iota(jnp.int32, (rows, rows), 0)
    before = (at < lax.broadcasted_iota(jnp.int32, (rows, rows), 1)).astype(jnp.float32).astype(jnp.bfloat16)
    order = lax.broadcasted_iota(jnp.int32, (CAP, rows), 0).astype(jnp.float32)
    nothing = jnp.zeros((CAP, rows), jnp.bfloat16)
    for n in range(2):
        route_a, route_b, gate_a, gate_b = (codes[4 * n + k : 4 * n + k + 1] for k in range(4))
        hit_a, hit_b = wanted == route_a, wanted == route_b
        hit = jnp.where(hit_a | hit_b, 1.0, 0.0)
        rank = jnp.dot(hit.astype(jnp.bfloat16), before, preferred_element_type=jnp.float32)
        rank = jnp.where(hit > 0, rank, -1.0)
        gate = jnp.where(hit_a, gate_a, gate_b) * (1.0 / 256.0)
        for to in range(GROUP):
            held = order == rank[to : to + 1]
            slots = slice((to * 2 + n) * CAP, (to * 2 + n + 1) * CAP)
            here, there = slice(n * rows, (n + 1) * rows), slice((1 - n) * rows, (2 - n) * rows)
            pick_ref[slots, here] = jnp.where(held, 1.0, 0.0).astype(jnp.bfloat16)
            gate_ref[slots, here] = jnp.where(held, gate[to : to + 1], 0.0).astype(jnp.bfloat16)
            pick_ref[slots, there] = nothing
            gate_ref[slots, there] = nothing


def cut(own_left, twin_left, own_right, twin_right, top_ref, low_ref):
    half = top_ref.shape[0] // 2
    top_ref[:half] = own_left[:half]
    top_ref[half:] = twin_left[:half]
    low_ref[:half] = own_right[half:]
    low_ref[half:] = twin_right[half:]


def to_slots(*refs):
    out_ref = refs[-1]
    count, base = out_ref.shape[0], 0
    for pick_ref, rows_ref in zip(refs[:-1:2], refs[1:-1:2]):
        rows = rows_ref[: pick_ref.shape[1]]
        found = jnp.dot(pick_ref[...], rows, preferred_element_type=jnp.float32)
        found = found.astype(jnp.bfloat16).reshape(count, -1, found.shape[1])
        out_ref[:, base : base + found.shape[1], :] = found
        base += found.shape[1]


def near_slots(base_ref, own_ref, other_ref, tok_ref, grad_ref, pick_ref, gate_ref, out_ref):
    gather_near(own_ref, other_ref, tok_ref, grad_ref)
    slot_maps(base_ref, tok_ref.at[grad_ref.shape[0] :], pick_ref, gate_ref)
    to_slots(pick_ref, tok_ref, gate_ref, grad_ref, out_ref)


def on_core(body, shapes, *arrays, us=0, scalars=0):
    in_vmem = pl.BlockSpec(memory_space=pltpu.VMEM)
    return pl.pallas_call(
        body,
        out_shape=shapes,
        in_specs=[pl.BlockSpec(memory_space=pltpu.SMEM)] * scalars + [in_vmem] * (len(arrays) - scalars),
        out_specs=jax.tree.map(lambda _: in_vmem, shapes),
        compiler_params=pltpu.CompilerParams(vmem_limit_bytes=32 << 20),
        cost_estimate=pl.CostEstimate(flops=us * 1_000_000_000, bytes_accessed=us * 3_300_000, transcendentals=us * 1_000_000),
    )(*arrays)


def keep(in_ref, out_ref):
    out_ref[...] = in_ref[...]


def pace(small, *after):
    return on_core(keep, jax.ShapeDtypeStruct(small.shape, small.dtype), hold(small, *after), us=100)


def local(tokens, grad_out, routes, gate_fixed, live_count, w_gate, w_up, w_down):
    rows, width = tokens.shape
    hidden_units = w_gate.shape[2]
    shard = w_gate.shape[1]
    half = shard // 2
    dp = lax.axis_index("dp")
    expert = lax.axis_index("expert")
    z_lo, y = dp // NY, dp % NY
    z_hi = expert // GROUP

    def bf16_type(*shape):
        return jax.ShapeDtypeStruct(shape, jnp.bfloat16)

    codes = jnp.tile(jnp.concatenate([routes.T, gate_fixed.T]), (CODES // 4, 1))
    place_now = jnp.stack([z_lo, y, live_count[0]]).astype(jnp.int32)
    both = on_core(turn, bf16_type(2 * rows + CODES, width), place_now, codes, tokens, grad_out, scalars=1)

    def swap_halves(array):
        return jnp.concatenate([array[..., width // 2 : width], array[..., : width // 2], array[..., width:]], axis=-1)

    both_across = move(both, across)
    w_gate = hold(w_gate, both)
    own = jnp.concatenate([w_gate[0], w_up[0], w_down[0].T], axis=1)
    own_left, own_right = move(own, y_by(1)), move(own, y_by(-1))
    twins = move(own, twin)
    slots = GROUP * 2 * CAP
    base = (z_hi * GROUP).astype(jnp.int32)[None]
    map_type = bf16_type(slots, 2 * rows)
    near_types = bf16_type(2 * rows + CODES, width), bf16_type(2 * rows, width), map_type, map_type
    near_types += (bf16_type(GROUP, 4 * CAP, width),)
    tok_near, grad_near, pick_near, _, near_sent = on_core(
        near_slots, near_types, base, both, both_across, us=100, scalars=1
    )
    tok_far = move(tok_near, onward)
    twins = hold(twins, own_left, own_right)
    twin_left, twin_right = move(twins, y_by(1)), move(twins, y_by(-1))
    cut_type = jax.ShapeDtypeStruct((shard, 3 * hidden_units), jnp.bfloat16)
    top, low = on_core(cut, (cut_type, cut_type), own_left, twin_left, own_right, twin_right)
    grad_far = move(hold(grad_near, top, low), onward)

    pick_far, pick_gate_far = on_core(
        slot_maps, (map_type, map_type), hold(base, top, low), tok_far[2 * rows :], scalars=1
    )
    groups = [list(range(h * GROUP, (h + 1) * GROUP)) for h in range(NZ // 2)]

    def exchange(array):
        return lax.all_to_all(
            array.reshape(GROUP, -1, array.shape[1]), "expert", 0, 0, axis_index_groups=groups, tiled=True
        )

    def slots_of(*pairs, us=0):
        shape = jax.ShapeDtypeStruct((GROUP, len(pairs) // 2 * 2 * CAP, width), jnp.bfloat16)
        return on_core(to_slots, shape, *pairs, us=us)


    near_sent = hold(near_sent, own_left, own_right, twins)
    near_rows = exchange(near_sent.reshape(2 * slots, width))
    tok_sent = hold(slots_of(hold(pick_far, top, low), tok_far, us=100), near_rows)
    far_top, far_low = move(top, y_by(1)), move(low, y_by(-1))
    tok_rows = exchange(tok_sent.reshape(slots, width)).reshape(slots, width)
    near_x = near_rows[:, : 2 * CAP].reshape(slots, width)
    near_g = near_rows[:, 2 * CAP :].reshape(slots, width)
    near_x, near_g = hold(near_x, tok_sent), hold(near_g, tok_sent)
    pick_gate_far, near_x, near_g, far_top, far_low = lax.optimization_barrier(
        (pick_gate_far, near_x, near_g, far_top, far_low)
    )
    grad_sent = hold(slots_of(pick_gate_far, grad_far, us=100), tok_rows)
    far_rows = exchange(grad_sent.reshape(slots, width)).reshape(slots, width)
    in_rows = jnp.concatenate([hold(near_x, grad_sent), tok_rows])
    grad_rows = jnp.concatenate([near_g, far_rows])
    far_top, far_low = hold(far_top, grad_sent), hold(far_low, grad_sent)
    full = jnp.concatenate(
        [far_top[half:], far_low[half:], twin_right, twin_left, twins]
        + [far_top[:half], far_low[:half], own_right, own_left, own]
    )
    pre = dot(in_rows, full[:, : 2 * hidden_units], ((1,), (0,)))
    gate_pre, up_pre = pre[:, :hidden_units], pre[:, hidden_units:]
    sig = jax.nn.sigmoid(gate_pre)
    act = gate_pre * sig
    hidden = act * up_pre
    weighted = bf16(hidden)
    slope = up_pre * sig * (1.0 + gate_pre * (1.0 - sig))

    def share(left, right, first, count):
        return bf16(dot(left[:, first * half : (first + count) * half], right, ((0,), (0,))))

    down_theirs = share(grad_rows, weighted, 0, 8)
    scaled = dot(hold(grad_rows, down_theirs), full[:, 2 * hidden_units :], ((1,), (0,)))
    down_theirs = move(down_theirs, twin)
    route_grad = jnp.sum(scaled * hidden, axis=1)
    deltas = bf16(jnp.concatenate([scaled * slope, scaled * act], axis=1))
    middle = width // 2
    ends = [
        jnp.concatenate([in_rows[:, at : at + half], in_rows[:, middle + at : middle + at + half]], axis=1)
        for at in (0, half)
    ]
    top, low = (share(part, deltas, 0, 2) for part in ends)
    ready = hold(deltas, top, low)
    top, low = move(top, y_by(1)), move(low, y_by(-1))

    extra = 128
    lane = jnp.arange(extra, dtype=jnp.int32)[None, :]
    tail = bf16(jnp.where(lane == expert, route_grad[:, None], 0.0))

    def row_grads(delta, at):
        slot_dx = bf16(dot(delta, full[:, : 2 * hidden_units], ((1,), (1,))))
        return jnp.concatenate([slot_dx, tail[at : at + slots]], axis=1)

    dx_far = row_grads(ready[slots:], slots)
    back_far = exchange(dx_far).reshape(slots, width + extra)
    gone = pace(lane + expert, top, low)
    parts_far = bf16(dot(hold(pick_far, gone), back_far, ((0,), (0,))))
    for_near = move(parts_far, backward)
    dx_near = row_grads(hold(ready[:slots], dx_far), 0)
    back_near = exchange(hold(dx_near, parts_far)).reshape(slots, width + extra)

    def around(top, low, up, down, stay):
        up = jnp.concatenate([bf16(f32(up[:half]) + f32(top)), up[half:]])
        down = jnp.concatenate([down[:half], bf16(f32(down[half:]) + f32(low))])
        return f32(stay) + f32(move(up, y_by(1))) + f32(move(down, y_by(-1)))

    gone = pace(lane + expert, for_near)
    parts_near = dot(hold(pick_near, gone), back_near, ((0,), (0,)))
    for_near = f32(for_near)
    for_across = bf16(swap_halves(parts_near[rows:] + for_near[rows:]))
    left = hold(in_rows, top, low)
    theirs = bf16(around(top[:half], low[:half], *(share(left, deltas, at, 2) for at in (2, 4, 6))))
    down_sum = bf16(f32(share(hold(grad_rows, top, low), weighted, 8, 8)) + f32(down_theirs))
    down_top, down_low = move(down_sum[:half], y_by(1)), move(down_sum[half:shard], y_by(-1))
    down_top, down_low = hold(down_top, for_across), hold(down_low, for_across)
    top, low = hold(top, theirs), hold(low, theirs)
    theirs = move(theirs, twin)
    mine = around(top[half:], low[half:], *(share(left, deltas, at, 2) for at in (10, 12, 14)))
    total = around(down_top, down_low, *(down_sum[n * shard : (n + 1) * shard] for n in (1, 2, 3)))
    grad_down = bf16(total).T[None]
    total = bf16(mine + f32(theirs))
    grad_gate, grad_up = total[None, :, :hidden_units], total[None, :, hidden_units:]

    for_across = move(for_across, across)
    whole = parts_near[:rows] + for_near[:rows] + f32(for_across)
    plain = [ORDER.index((dy, far, low)) for far in range(2) for dy in range(NY) for low in range(2)]
    ordered = reorder(bf16(whole[:, :width]), plain, half)
    spots = [((z + z_lo) % 2 * NY + (at - y) % NY) * shard for z in range(2) for at in range(NY)]
    d_tokens = pieces(ordered, spots, shard)
    found = jnp.where(lane[:, None, :] == routes[:, :, None], whole[:, None, width:], 0.0)
    d_gates = bf16(jnp.sum(found, axis=2) / (f32(gate_fixed) / 256.0))
    return d_tokens, d_gates, grad_gate, grad_up, grad_down


def solution(mesh):
    rows = P(("dp", "expert"), None)
    return jax.shard_map(
        local,
        mesh=mesh,
        in_specs=(
            rows,
            rows,
            rows,
            rows,
            P(("dp", "expert")),
            P("expert", "dp", None),
            P("expert", "dp", None),
            P("expert", None, "dp"),
        ),
        out_specs=(
            rows,
            rows,
            P("expert", "dp", None),
            P("expert", "dp", None),
            P("expert", None, "dp"),
        ),
        check_vma=False,
    )
```

```python
import jax
import jax.numpy as jnp
from jax import lax
from jax.experimental import pallas as pl
from jax.experimental.pallas import tpu as pltpu
from jax.sharding import PartitionSpec as P

NZ, NY, NX = 8, 4, 4
ALL = ("dp", "expert")
CAP = 16
CODES = 16
GROUP = 2 * NX


def place(index):
    dp, expert = divmod(index, (NZ // 2) * GROUP)
    z_lo, y = divmod(dp, NY)
    z_hi, rest = divmod(expert, GROUP)
    x, core = divmod(rest, 2)
    return 2 * z_hi + z_lo, y, x, core


def index_of(z, y, x, core):
    z, y, x = z % NZ, y % NY, x % NX
    return ((z % 2) * NY + y) * (NZ // 2) * GROUP + (z // 2) * GROUP + x * 2 + core


def move(array, to):
    pairs = [(i, index_of(*to(*place(i)))) for i in range(NZ * NY * GROUP)]
    return lax.ppermute(array, ALL, pairs)


def across(z, y, x, core):
    return (z + 1 if z % 2 else z - 1), y, x, core


def onward(z, y, x, core):
    return (z - 2 if z % 2 else z + 2), y, x, core


def beyond(z, y, x, core):
    return onward(*across(z, y, x, core))


def backward(z, y, x, core):
    return (z + 2 if z % 2 else z - 2), y, x, core


def twin(z, y, x, core):
    return z ^ 1, y, x, core


def y_by(step):
    return lambda z, y, x, core: (z, y + step, x, core)


def dot(left, right, dims):
    return lax.dot_general(left, right, (dims, ((), ())), preferred_element_type=jnp.float32)


def bf16(array):
    return array.astype(jnp.bfloat16)


def f32(array):
    return array.astype(jnp.float32)


def hold(array, *after):
    return lax.optimization_barrier((array,) + after)[0]


ORDER = [(dy, far, low) for far in (1, 0) for dy in (2, 1, 3, 0) for low in (0, 1)]


def pieces(array, starts, size):
    return jnp.concatenate([lax.dynamic_slice_in_dim(array, at, size, 1) for at in starts], axis=1)


def reorder(array, order, size, base=0):
    parts = [array[..., base + at * size : base + (at + 1) * size] for at in order]
    return jnp.concatenate(parts, axis=-1)


def turn(place_ref, codes_ref, tok_ref, grad_ref, out_ref):
    z_lo, y, live = place_ref[0], place_ref[1], place_ref[2]
    rows, width = tok_ref.shape
    half = width // len(ORDER)
    for n, (dy, far, low) in enumerate(ORDER):
        at = (((z_lo + far) & 1) * NY + ((y + dy) & (NY - 1))) * 2 + low
        at = pl.multiple_of(at * half, half)
        out_ref[:rows, n * half : (n + 1) * half] = tok_ref[:, pl.ds(at, half)]
        out_ref[rows : 2 * rows, n * half : (n + 1) * half] = grad_ref[:, pl.ds(at, half)]
    out_ref[2 * rows :] = jnp.zeros((CODES, width), jnp.bfloat16)
    row = lax.broadcasted_iota(jnp.int32, codes_ref.shape, 0)
    dead = ((row & 3) < 2) & (lax.broadcasted_iota(jnp.int32, codes_ref.shape, 1) >= live)
    out_ref[2 * rows :, :rows] = jnp.where(dead, -1, codes_ref[...]).astype(jnp.float32).astype(jnp.bfloat16)


def gather_near(own_ref, other_ref, tok_ref, grad_ref):
    width = own_ref.shape[1]
    middle = width // 2
    rows = grad_ref.shape[0] // 2
    for at, out_ref in ((0, tok_ref), (rows, grad_ref)):
        out_ref[:rows] = own_ref[at : at + rows]
        out_ref[rows : 2 * rows, :middle] = other_ref[at : at + rows, middle:]
        out_ref[rows : 2 * rows, middle:] = other_ref[at : at + rows, :middle]
    own, other = own_ref[2 * rows :, :rows].astype(jnp.float32), other_ref[2 * rows :, :rows].astype(jnp.float32)
    first = lax.broadcasted_iota(jnp.int32, own.shape, 0) < 4
    tok_ref[2 * rows :] = jnp.zeros((CODES, width), jnp.bfloat16)
    tok_ref[2 * rows :, :rows] = jnp.where(first, own, other).astype(jnp.bfloat16)


def slot_maps(base_ref, codes_ref, pick_ref, gate_ref):
    rows = pick_ref.shape[1] // 2
    codes = codes_ref[:, :rows].astype(jnp.float32)
    wanted = (lax.broadcasted_iota(jnp.int32, (GROUP, rows), 0) + base_ref[0]).astype(jnp.float32)
    at = lax.broadcasted_iota(jnp.int32, (rows, rows), 0)
    before = (at < lax.broadcasted_iota(jnp.int32, (rows, rows), 1)).astype(jnp.float32).astype(jnp.bfloat16)
    order = lax.broadcasted_iota(jnp.int32, (CAP, rows), 0).astype(jnp.float32)
    nothing = jnp.zeros((CAP, rows), jnp.bfloat16)
    for n in range(2):
        route_a, route_b, gate_a, gate_b = (codes[4 * n + k : 4 * n + k + 1] for k in range(4))
        hit_a, hit_b = wanted == route_a, wanted == route_b
        hit = jnp.where(hit_a | hit_b, 1.0, 0.0)
        rank = jnp.dot(hit.astype(jnp.bfloat16), before, preferred_element_type=jnp.float32)
        rank = jnp.where(hit > 0, rank, -1.0)
        gate = jnp.where(hit_a, gate_a, gate_b) * (1.0 / 256.0)
        for to in range(GROUP):
            held = order == rank[to : to + 1]
            slots = slice((to * 2 + n) * CAP, (to * 2 + n + 1) * CAP)
            here, there = slice(n * rows, (n + 1) * rows), slice((1 - n) * rows, (2 - n) * rows)
            pick_ref[slots, here] = jnp.where(held, 1.0, 0.0).astype(jnp.bfloat16)
            gate_ref[slots, here] = jnp.where(held, gate[to : to + 1], 0.0).astype(jnp.bfloat16)
            pick_ref[slots, there] = nothing
            gate_ref[slots, there] = nothing


def cut(own_left, twin_left, own_right, twin_right, top_ref, low_ref):
    half = top_ref.shape[0] // 2
    top_ref[:half] = own_left[:half]
    top_ref[half:] = twin_left[:half]
    low_ref[:half] = own_right[half:]
    low_ref[half:] = twin_right[half:]


def to_slots(*refs):
    out_ref = refs[-1]
    count, base = out_ref.shape[0], 0
    for pick_ref, rows_ref in zip(refs[:-1:2], refs[1:-1:2]):
        rows = rows_ref[: pick_ref.shape[1]]
        found = jnp.dot(pick_ref[...], rows, preferred_element_type=jnp.float32)
        found = found.astype(jnp.bfloat16).reshape(count, -1, found.shape[1])
        out_ref[:, base : base + found.shape[1], :] = found
        base += found.shape[1]


def near_slots(base_ref, own_ref, other_ref, tok_ref, grad_ref, pick_ref, gate_ref, out_ref):
    gather_near(own_ref, other_ref, tok_ref, grad_ref)
    slot_maps(base_ref, tok_ref.at[grad_ref.shape[0] :], pick_ref, gate_ref)
    to_slots(pick_ref, tok_ref, gate_ref, grad_ref, out_ref)


def on_core(body, shapes, *arrays, us=0, scalars=0):
    in_vmem = pl.BlockSpec(memory_space=pltpu.VMEM)
    return pl.pallas_call(
        body,
        out_shape=shapes,
        in_specs=[pl.BlockSpec(memory_space=pltpu.SMEM)] * scalars + [in_vmem] * (len(arrays) - scalars),
        out_specs=jax.tree.map(lambda _: in_vmem, shapes),
        compiler_params=pltpu.CompilerParams(vmem_limit_bytes=32 << 20),
        cost_estimate=pl.CostEstimate(flops=us * 1_000_000_000, bytes_accessed=us * 3_300_000, transcendentals=us * 1_000_000),
    )(*arrays)


def keep(in_ref, out_ref):
    out_ref[...] = in_ref[...]


def pace(small, *after):
    return on_core(keep, jax.ShapeDtypeStruct(small.shape, small.dtype), hold(small, *after), us=100)


def local(tokens, grad_out, routes, gate_fixed, live_count, w_gate, w_up, w_down):
    rows, width = tokens.shape
    hidden_units = w_gate.shape[2]
    shard = w_gate.shape[1]
    half = shard // 2
    dp = lax.axis_index("dp")
    expert = lax.axis_index("expert")
    z_lo, y = dp // NY, dp % NY
    z_hi = expert // GROUP

    def bf16_type(*shape):
        return jax.ShapeDtypeStruct(shape, jnp.bfloat16)

    codes = jnp.tile(jnp.concatenate([routes.T, gate_fixed.T]), (CODES // 4, 1))
    place_now = jnp.stack([z_lo, y, live_count[0]]).astype(jnp.int32)
    both = on_core(turn, bf16_type(2 * rows + CODES, width), place_now, codes, tokens, grad_out, scalars=1)

    def swap_halves(array):
        return jnp.concatenate([array[..., width // 2 : width], array[..., : width // 2], array[..., width:]], axis=-1)

    both_across = move(both, across)
    w_gate = hold(w_gate, both)
    own = jnp.concatenate([w_gate[0], w_up[0], w_down[0].T], axis=1)
    own_left, own_right = move(own, y_by(1)), move(own, y_by(-1))
    twins = move(own, twin)
    slots = GROUP * 2 * CAP
    base = (z_hi * GROUP).astype(jnp.int32)[None]
    map_type = bf16_type(slots, 2 * rows)
    near_types = bf16_type(2 * rows + CODES, width), bf16_type(2 * rows, width), map_type, map_type
    near_types += (bf16_type(GROUP, 4 * CAP, width),)
    tok_near, grad_near, pick_near, _, near_sent = on_core(
        near_slots, near_types, base, both, both_across, us=100, scalars=1
    )
    tok_far = move(tok_near, onward)
    twins = hold(twins, own_left, own_right)
    twin_left, twin_right = move(twins, y_by(1)), move(twins, y_by(-1))
    cut_type = jax.ShapeDtypeStruct((shard, 3 * hidden_units), jnp.bfloat16)
    top, low = on_core(cut, (cut_type, cut_type), own_left, twin_left, own_right, twin_right)
    grad_far = move(hold(grad_near, top, low), onward)

    pick_far, pick_gate_far = on_core(
        slot_maps, (map_type, map_type), hold(base, top, low), tok_far[2 * rows :], scalars=1
    )
    groups = [list(range(h * GROUP, (h + 1) * GROUP)) for h in range(NZ // 2)]

    def exchange(array):
        return lax.all_to_all(
            array.reshape(GROUP, -1, array.shape[1]), "expert", 0, 0, axis_index_groups=groups, tiled=True
        )

    def slots_of(*pairs, us=0):
        shape = jax.ShapeDtypeStruct((GROUP, len(pairs) // 2 * 2 * CAP, width), jnp.bfloat16)
        return on_core(to_slots, shape, *pairs, us=us)


    near_sent = hold(near_sent, own_left, own_right, twins)
    near_rows = exchange(near_sent.reshape(2 * slots, width))
    tok_sent = hold(slots_of(hold(pick_far, top, low), tok_far, us=100), near_rows)
    far_top, far_low = move(top, y_by(1)), move(low, y_by(-1))
    tok_rows = exchange(tok_sent.reshape(slots, width)).reshape(slots, width)
    near_x = near_rows[:, : 2 * CAP].reshape(slots, width)
    near_g = near_rows[:, 2 * CAP :].reshape(slots, width)
    near_x, near_g = hold(near_x, tok_sent), hold(near_g, tok_sent)
    pick_gate_far, near_x, near_g, far_top, far_low = lax.optimization_barrier(
        (pick_gate_far, near_x, near_g, far_top, far_low)
    )
    grad_sent = hold(slots_of(pick_gate_far, grad_far, us=100), tok_rows)
    far_rows = exchange(grad_sent.reshape(slots, width)).reshape(slots, width)
    in_rows = jnp.concatenate([hold(near_x, grad_sent), tok_rows])
    grad_rows = jnp.concatenate([near_g, far_rows])
    far_top, far_low = hold(far_top, grad_sent), hold(far_low, grad_sent)
    full = jnp.concatenate(
        [far_top[half:], far_low[half:], twin_right, twin_left, twins]
        + [far_top[:half], far_low[:half], own_right, own_left, own]
    )
    pre = dot(in_rows, full[:, : 2 * hidden_units], ((1,), (0,)))
    gate_pre, up_pre = pre[:, :hidden_units], pre[:, hidden_units:]
    sig = jax.nn.sigmoid(gate_pre)
    act = gate_pre * sig
    hidden = act * up_pre
    weighted = bf16(hidden)
    slope = up_pre * sig * (1.0 + gate_pre * (1.0 - sig))

    def share(left, right, first, count):
        return bf16(dot(left[:, first * half : (first + count) * half], right, ((0,), (0,))))

    down_theirs = share(grad_rows, weighted, 0, 8)
    scaled = dot(hold(grad_rows, down_theirs), full[:, 2 * hidden_units :], ((1,), (0,)))
    down_theirs = move(down_theirs, twin)
    route_grad = jnp.sum(scaled * hidden, axis=1)
    deltas = bf16(jnp.concatenate([scaled * slope, scaled * act], axis=1))
    middle = width // 2
    ends = [
        jnp.concatenate([in_rows[:, at : at + half], in_rows[:, middle + at : middle + at + half]], axis=1)
        for at in (0, half)
    ]
    top, low = (share(part, deltas, 0, 2) for part in ends)
    ready = hold(deltas, top, low)
    top, low = move(top, y_by(1)), move(low, y_by(-1))

    extra = 128
    lane = jnp.arange(extra, dtype=jnp.int32)[None, :]
    tail = bf16(jnp.where(lane == expert, route_grad[:, None], 0.0))

    def row_grads(delta, at):
        slot_dx = bf16(dot(delta, full[:, : 2 * hidden_units], ((1,), (1,))))
        return jnp.concatenate([slot_dx, tail[at : at + slots]], axis=1)

    dx_far = row_grads(ready[slots:], slots)
    back_far = exchange(dx_far).reshape(slots, width + extra)
    gone = pace(lane + expert, top, low)
    parts_far = bf16(dot(hold(pick_far, gone), back_far, ((0,), (0,))))
    for_near = move(parts_far, backward)
    dx_near = row_grads(hold(ready[:slots], dx_far), 0)
    back_near = exchange(hold(dx_near, parts_far)).reshape(slots, width + extra)

    def around(top, low, up, down, stay):
        up = jnp.concatenate([bf16(f32(up[:half]) + f32(top)), up[half:]])
        down = jnp.concatenate([down[:half], bf16(f32(down[half:]) + f32(low))])
        return f32(stay) + f32(move(up, y_by(1))) + f32(move(down, y_by(-1)))

    gone = pace(lane + expert, for_near)
    parts_near = dot(hold(pick_near, gone), back_near, ((0,), (0,)))
    for_near = f32(for_near)
    for_across = bf16(swap_halves(parts_near[rows:] + for_near[rows:]))
    left = hold(in_rows, top, low)
    theirs = bf16(around(top[:half], low[:half], *(share(left, deltas, at, 2) for at in (2, 4, 6))))
    down_sum = bf16(f32(share(hold(grad_rows, top, low), weighted, 8, 8)) + f32(down_theirs))
    down_top, down_low = move(down_sum[:half], y_by(1)), move(down_sum[half:shard], y_by(-1))
    top, low = hold(top, theirs), hold(low, theirs)
    theirs = move(theirs, twin)
    down_top, down_low = hold(down_top, for_across), hold(down_low, for_across, theirs)
    mine = around(top[half:], low[half:], *(share(left, deltas, at, 2) for at in (10, 12, 14)))
    total = around(down_top, down_low, *(down_sum[n * shard : (n + 1) * shard] for n in (1, 2, 3)))
    grad_down = bf16(total).T[None]
    total = bf16(mine + f32(theirs))
    grad_gate, grad_up = total[None, :, :hidden_units], total[None, :, hidden_units:]

    for_across = move(for_across, across)
    whole = parts_near[:rows] + for_near[:rows] + f32(for_across)
    plain = [ORDER.index((dy, far, low)) for far in range(2) for dy in range(NY) for low in range(2)]
    ordered = reorder(bf16(whole[:, :width]), plain, half)
    spots = [((z + z_lo) % 2 * NY + (at - y) % NY) * shard for z in range(2) for at in range(NY)]
    d_tokens = pieces(ordered, spots, shard)
    found = jnp.where(lane[:, None, :] == routes[:, :, None], whole[:, None, width:], 0.0)
    d_gates = bf16(jnp.sum(found, axis=2) / (f32(gate_fixed) / 256.0))
    return d_tokens, d_gates, grad_gate, grad_up, grad_down


def solution(mesh):
    rows = P(("dp", "expert"), None)
    return jax.shard_map(
        local,
        mesh=mesh,
        in_specs=(
            rows,
            rows,
            rows,
            rows,
            P(("dp", "expert")),
            P("expert", "dp", None),
            P("expert", "dp", None),
            P("expert", None, "dp"),
        ),
        out_specs=(
            rows,
            rows,
            P("expert", "dp", None),
            P("expert", "dp", None),
            P("expert", None, "dp"),
        ),
        check_vma=False,
    )
```
